512 devices in a mesh: row: 4 (over x), col: 16 (over z), layer: 8 (over y, core).
Axes of the slice: x: 4, y: 4, z: 16, core: 2. Of those that a mesh axis runs over, the one named last changes fastest.
Arguments:
- a_blocks: bfloat16 [4, 16, 8, 24, 128, 128], P('row', 'col', 'layer'), may hold values from -6 to 6
- a_cells: int32 [4, 16, 8, 24], P('row', 'col', 'layer'), may hold values from 0 to 31, as said below
- a_count: int32 [4, 16, 8], P('row', 'col', 'layer'), may hold values from 12 to 24, as said below
- b_blocks: bfloat16 [4, 16, 8, 80, 128, 128], P('row', 'col', 'layer'), may hold values from -0.0625 to 0.0625
- b_cells: int32 [4, 16, 8, 80], P('row', 'col', 'layer'), may hold values from 0 to 127, as said below
- b_count: int32 [4, 16, 8], P('row', 'col', 'layer'), may hold values from 40 to 80, as said below
- c_cells: int32 [4, 16, 32], P('row', 'col'), may hold values from 0 to 63, as said below
Outputs:
- c_blocks: float32 [4, 16, 32, 128, 128], P('row', 'col', 'layer')
The draws below stay inside these ranges and needn't reach their ends.
Inputs may be any that keep to these rules, and one draw needn't show every extreme that they name: `a_cells`: positions are distinct within each A panel. `a_count`: some panel is full in every draw. `b_cells`: positions are distinct within each B panel. `b_count`: some panel is full in every draw. `c_cells`: positions are distinct within each tile.
All inputs are finite; a program needn't handle non-finite values.
Results may differ from the reference program's by a relative error of at most 0.0003.
Values may be sent and summed in bfloat16 or wider, within the bound.
A program may use at most 128 MiB of HBM per device.

```python
import jax
import jax.numpy as jnp
from jax import lax

BS = 128
CR = 4
CC = 16
KW = 8
CAP_A = 24
CAP_B = 80
CAP_C = 32
N_ROW = 4
N_COL = 16
N_LAYER = 8


def panel_cells(key, panels, positions, capacity):
    subkeys = jax.random.split(key, panels)
    return jax.vmap(lambda subkey: jax.random.permutation(subkey, positions)[:capacity])(subkeys).astype(jnp.int32)


def live_counts(key, capacity):
    panels = N_ROW * N_COL * N_LAYER
    drawn_counts = jax.random.randint(jax.random.fold_in(key, 1), (panels,), capacity // 2, capacity + 1)
    full_panel = jax.random.randint(jax.random.fold_in(key, 2), (), 0, panels)
    counts_out = jnp.where(jnp.arange(panels) == full_panel, capacity, drawn_counts)
    return counts_out.astype(jnp.int32).reshape(N_ROW, N_COL, N_LAYER)


def draw_a_cells(key, part):
    cell_lists = panel_cells(jax.random.fold_in(key, 101), N_ROW * N_COL * N_LAYER, CR * KW, CAP_A)
    return cell_lists.reshape(N_ROW, N_COL, N_LAYER, CAP_A)


def draw_b_cells(key, part):
    cell_lists = panel_cells(jax.random.fold_in(key, 102), N_ROW * N_COL * N_LAYER, KW * CC, CAP_B)
    return cell_lists.reshape(N_ROW, N_COL, N_LAYER, CAP_B)


def draw_c_cells(key, part):
    cell_lists = panel_cells(jax.random.fold_in(key, 103), N_ROW * N_COL, CR * CC, CAP_C)
    return cell_lists.reshape(N_ROW, N_COL, CAP_C)


def draw_a_count(key, part):
    return live_counts(jax.random.fold_in(key, 201), CAP_A)


def draw_b_count(key, part):
    return live_counts(jax.random.fold_in(key, 301), CAP_B)


def block_levels(rng, dims, cuts, low, top_value):
    gain, own = 1.0, jax.random.fold_in(rng, 6)
    for position, parts in cuts:
        draws = jnp.exp(jax.random.uniform(jax.random.fold_in(own, position), (parts,), jnp.float32, low / len(cuts), top_value / len(cuts)))
        gain = gain * jnp.repeat(draws, dims[position] // parts).reshape([-1 if axis == position else 1 for axis in range(len(dims))])
    return gain


def scatter_about(stream_key, dims, deviation, most, cuts=(), kind=jnp.bfloat16):
    factor_of = block_levels(stream_key, dims, cuts, -0.22, 0.18) if cuts else 1.0
    values = jax.random.normal(stream_key, dims, jnp.float32) * deviation * factor_of
    return jnp.minimum(jnp.maximum(values, -most), most).astype(kind)


def setup_inputs(seed: int = 0) -> dict:
    key_of = jax.random.split(jax.random.key(seed), 8)
    a_blocks = scatter_about(key_of[0], (N_ROW, N_COL, N_LAYER, CAP_A, BS, BS), 1.0, 6.0, ((0, 4), (1, 16), (2, 8)))
    a_cells = draw_a_cells(jax.random.fold_in(key_of[7], 71), 0)
    a_count = draw_a_count(jax.random.fold_in(key_of[7], 71), 0)
    b_blocks = scatter_about(key_of[3], (N_ROW, N_COL, N_LAYER, CAP_B, BS, BS), (N_LAYER * KW * BS) ** -0.5, 0.0625, ((0, 4), (1, 16), (2, 8)))
    b_cells = draw_b_cells(jax.random.fold_in(key_of[7], 71), 0)
    b_count = draw_b_count(jax.random.fold_in(key_of[7], 71), 0)
    c_cells = draw_c_cells(jax.random.fold_in(key_of[7], 71), 0)
    return dict(a_blocks=a_blocks, a_cells=a_cells, a_count=a_count, b_blocks=b_blocks, b_cells=b_cells, b_count=b_count, c_cells=c_cells)


def densify(blocks, cell_list, live_count, height, breadth):
    capacity = cell_list.shape[0]
    is_live = jnp.arange(capacity, dtype=jnp.int32) < live_count
    masked = jnp.where(is_live[:, None, None], blocks, jnp.zeros((), blocks.dtype))
    filled = jnp.zeros((height * breadth,) + blocks.shape[1:], blocks.dtype)
    filled = filled.at[cell_list.astype(jnp.int32)].add(masked)
    return filled.reshape(height, breadth, blocks.shape[1], blocks.shape[2])


def stop_product(left, right):
    return jnp.einsum("ikxz,kjzy->ijxy", left.astype(jnp.float32), right.astype(jnp.float32), precision=lax.Precision.HIGHEST)


def reference(a_blocks, a_cells, a_count, b_blocks, b_cells, b_count, c_cells):
    def one_tile(flat_index):
        row_index = (flat_index // N_COL).astype(jnp.int32)
        col_index = (flat_index % N_COL).astype(jnp.int32)
        row_next = ((row_index + 1) % N_ROW).astype(jnp.int32)
        col_next = ((col_index + 1) % N_COL).astype(jnp.int32)
        summed = jnp.zeros((CAP_C, BS, BS), jnp.float32)
        for layer in range(N_LAYER):
            left_here = densify(a_blocks[row_index, col_index, layer], a_cells[row_index, col_index, layer], a_count[row_index, col_index, layer], CR, KW)
            right_here = densify(b_blocks[row_index, col_index, layer], b_cells[row_index, col_index, layer], b_count[row_index, col_index, layer], KW, CC)
            left_next = densify(a_blocks[row_next, col_index, layer], a_cells[row_next, col_index, layer], a_count[row_next, col_index, layer], CR, KW)
            right_next = densify(b_blocks[row_index, col_next, layer], b_cells[row_index, col_next, layer], b_count[row_index, col_next, layer], KW, CC)
            partial_value = stop_product(left_here, right_here) + stop_product(left_next, right_next)
            kept = jnp.take(partial_value.reshape(CR * CC, BS, BS), c_cells[row_index, col_index].astype(jnp.int32), axis=0)
            summed = summed + kept
        return summed

    tiles = lax.map(one_tile, jnp.arange(N_ROW * N_COL, dtype=jnp.int32))
    return tiles.reshape(N_ROW, N_COL, CAP_C, BS, BS)
```

```python
import jax
import jax.numpy as jnp
from jax import lax
from jax.experimental import pallas as pl
from jax.experimental.pallas import tpu as pltpu
from jax.sharding import PartitionSpec as P

CR = 4
CC = 16
KW = 8
BS = 128
ROWS1 = (32, 32, 32, 32)
ROWS2 = (32, 32, 32, 32)
MESH = pl.DeviceIdType.MESH
CORE, FA, FB, DA, DB, SA, SB, ZZ = range(8)


def plan_units():
    units = []
    for tile, rows in enumerate((ROWS1, ROWS2)):
        start = 0
        for part, height in enumerate(rows):
            units.append((tile, part, start, height))
            start += height
    return units


def plan_steps(first, total):
    steps = []
    for n in range(first + 3):
        if n < first:
            steps.append(("product", n))
        for lag, name in ((1, "chip"), (2, "forward"), (3, "finish")):
            if 0 <= n - lag < first:
                steps.append((name, n - lag))
    for n in range(first, total):
        steps.append(("product", n))
        if n > first:
            steps.append(("finish", n - 1))
        steps.append(("chip", n))
        if n > first:
            steps.append(("home", n - 1))
        steps.append(("forward", n))
    steps.append(("finish", total - 1))
    steps.append(("home", total - 1))
    return steps


def slot_table(cells, count, capacity):
    lanes = lax.broadcasted_iota(jnp.int32, (1, BS), 1)

    def place(s, table):
        cell = jnp.where(s < count, cells[0, 0, 0, s], -1)
        return jnp.where(lanes == cell, s, table)

    return lax.fori_loop(0, capacity, place, jnp.full((1, BS), capacity, jnp.int32), unroll=8)


def kernel(shape, a_cells, a_count, b_cells, b_count, c_cells, a_hbm, b_hbm, out, *scratch):
    n_row, n_col, n_layer = shape
    units = plan_units()
    parts = len(ROWS2)
    a_next = scratch[:parts]
    (a_own, b_slots, left, right, dense, kept, away, core_in,
     fa_in, fb_in, da_in, db_in, sa_in, sb_in, z_in,
     a_table, b_table, c_list, a_table_in, c_list_in,
     a_at, b_at, a_next_at, c_next_at,
     local_sem, a_send, a_recv, int_send, int_recv, send_sem, recv_sem) = scratch[parts:]
    cap_a = a_hbm.shape[3]
    cap_b = b_hbm.shape[3]

    r, c, l = lax.axis_index("row"), lax.axis_index("col"), lax.axis_index("layer")
    ny = n_layer // 2
    y, p = l // 2, l % 2
    r_up, r_down = lax.rem(r + 1, n_row), lax.rem(r + n_row - 1, n_row)
    c_up, c_down = lax.rem(c + 1, n_col), lax.rem(c + n_col - 1, n_col)
    a_to, a_from = (r_down, c_up, l), (r_up, c_down, l)
    sibling = (r, c, y * 2 + 1 - p)
    y_up = (r, c, lax.rem(y + 1, ny) * 2 + p)
    y_down = (r, c, lax.rem(y + ny - 1, ny) * 2 + p)
    z_up, z_down = (r, c_up, l), (r, c_down, l)

    barrier = pltpu.get_barrier_semaphore()
    others = (a_to, a_from, sibling, y_up, y_down, z_up, z_down)
    for other in others:
        pl.semaphore_signal(barrier, inc=1, device_id=other, device_id_type=MESH)

    b_copy = pltpu.make_async_copy(b_hbm.at[0, 0, 0], b_slots.at[pl.ds(0, cap_b)], local_sem.at[0])
    a_copy = pltpu.make_async_copy(a_hbm.at[0, 0, 0], a_own.at[pl.ds(0, cap_a)], local_sem.at[1])
    a_copy.start()
    b_copy.start()
    pl.semaphore_wait(barrier, len(others))

    def remote(src, dst, send, recv, device):
        return pltpu.make_async_remote_copy(
            src_ref=src, dst_ref=dst, send_sem=send, recv_sem=recv, device_id=device, device_id_type=MESH
        )

    a_copies = []
    for tile, part, start, height in units:
        if tile == 1:
            a_copies.append(
                remote(
                    a_hbm.at[0, 0, 0, :, pl.ds(start, height), :],
                    a_next[part].at[pl.ds(0, cap_a)],
                    a_send.at[part],
                    a_recv.at[part],
                    a_to,
                )
            )
    for copy in a_copies:
        copy.start()

    lanes = lax.broadcasted_iota(jnp.int32, (1, BS), 1)

    def list_cell(t, row):
        return jnp.where(lanes == t, c_cells[0, 0, t], row)

    a_table[...] = slot_table(a_cells, a_count[0, 0, 0], cap_a)
    a_at_copy = pltpu.make_async_copy(a_table, a_at, local_sem.at[2])
    a_at_copy.start()
    b_table[...] = slot_table(b_cells, b_count[0, 0, 0], cap_b)
    b_at_copy = pltpu.make_async_copy(b_table, b_at, local_sem.at[3])
    b_at_copy.start()
    a_table_copy = remote(a_table, a_table_in, int_send.at[0], int_recv.at[0], a_to)
    a_table_copy.start()
    c_list[...] = lax.fori_loop(0, c_cells.shape[2], list_cell, jnp.zeros((1, BS), jnp.int32), unroll=8)
    c_list_copy = remote(c_list, c_list_in, int_send.at[1], int_recv.at[1], z_up)
    c_list_copy.start()

    a_own[cap_a] = jnp.zeros((BS, BS), a_own.dtype)
    b_slots[cap_b] = jnp.zeros((BS, BS), b_slots.dtype)
    for tile, part, start, height in units:
        if tile == 1:
            a_next[part][cap_a] = jnp.zeros((height, BS), a_own.dtype)

    b_at_copy.wait()
    b_copy.wait()

    @pl.loop(0, KW)
    def _(k):
        for j in range(CC):
            right[j // 2, pl.ds(k * BS, BS), (j % 2) * BS:(j % 2 + 1) * BS] = b_slots[b_at[0, k * CC + j]]

    a_at_copy.wait()
    a_copy.wait()

    a_next_at_copy = pltpu.make_async_copy(a_table_in, a_next_at, local_sem.at[4])
    c_next_at_copy = pltpu.make_async_copy(c_list_in, c_next_at, local_sem.at[5])

    def copies_of(u):
        tile, part, start, height = units[u]
        rows = pl.ds(start, height)

        def link(kind, src, dst, device):
            return remote(src, dst, send_sem.at[u, kind], recv_sem.at[u, kind], device)

        def blocks(first, count):
            return kept.at[tile, pl.ds(first, count), rows, :]

        links = {
            CORE: link(CORE, away.at[tile, :, rows, :], core_in.at[tile, :, rows, :], sibling),
            FA: link(FA, blocks(8, 2), fa_in.at[tile, :, rows, :], y_up),
            FB: link(FB, blocks(10, 2), fb_in.at[tile, :, rows, :], y_down),
            DB: link(DB, blocks(6, 2), db_in.at[tile, :, rows, :], y_up),
            DA: link(DA, blocks(12, 2), da_in.at[tile, :, rows, :], y_down),
            SA: link(SA, blocks(4, 2), sa_in.at[tile, :, rows, :], y_up),
            SB: link(SB, blocks(14, 2), sb_in.at[tile, :, rows, :], y_down),
        }
        if tile == 1:
            links[ZZ] = link(ZZ, blocks(0, 4), z_in.at[:, rows, :], z_down)
        return links

    copies = [copies_of(u) for u in range(len(units))]

    def product(u):
        tile, part, start, height = units[u]
        rows = pl.ds(start, height)
        if tile == 1:
            if part == 0:
                a_table_copy.wait_recv()
                a_next_at_copy.start()
                c_list_copy.wait_recv()
                c_next_at_copy.start()
                a_next_at_copy.wait()
                c_next_at_copy.wait()
            a_copies[part].wait_recv()
        for i in range(CR):
            for k in range(KW):
                if tile == 0:
                    block = a_own[a_at[0, i * KW + k], rows, :]
                else:
                    block = a_next[part][a_next_at[0, i * KW + k]]
                left[i * height:(i + 1) * height, k * BS:(k + 1) * BS] = block

        @pl.loop(0, CC // 2)
        def _(j):
            total = jnp.dot(left[0:CR * height, :], right[j], preferred_element_type=jnp.float32)
            for i in range(CR):
                for s in range(2):
                    dense[i * CC + 2 * j + s, 0:height, :] = total[i * height:(i + 1) * height, s * BS:(s + 1) * BS]

        @pl.loop(0, ny)
        def _(e):
            base = lax.rem(y + e, ny) * 8
            for q in range(4):
                for ours, target in ((False, away), (True, kept)):
                    t = base + (p if ours else 1 - p) * 4 + q
                    cell = c_cells[0, 0, t] if tile == 0 else c_next_at[0, t]
                    target[tile, e * 4 + q, rows, :] = dense[cell, 0:height, :]

        copies[u][CORE].start()

    def chip(u):
        tile, part, start, height = units[u]
        rows = pl.ds(start, height)
        copies[u][CORE].wait_recv()
        for e, sends in ((2, (FA, FB)), (1, (DB,)), (3, (DA,)), (0, ())):
            span = slice(e * 4, e * 4 + 4)
            kept[tile, span, rows, :] += core_in[tile, span, rows, :]
            for kind in sends:
                copies[u][kind].start()

    def forward(u):
        tile, part, start, height = units[u]
        rows = pl.ds(start, height)
        for came, sent, first, arrived in ((FA, SA, 4, fa_in), (FB, SB, 14, fb_in)):
            copies[u][came].wait_recv()
            kept[tile, first:first + 2, rows, :] += arrived[tile, :, rows, :]
            copies[u][sent].start()

    def finish(u):
        tile, part, start, height = units[u]
        rows = pl.ds(start, height)
        for kind in (DA, DB, SA, SB):
            copies[u][kind].wait_recv()
        upper = kept[tile, 0:2, rows, :] + da_in[tile, :, rows, :] + sa_in[tile, :, rows, :]
        lower = kept[tile, 2:4, rows, :] + db_in[tile, :, rows, :] + sb_in[tile, :, rows, :]
        if tile == 0:
            out[0, 0, 0:2, rows, :] = upper
            out[0, 0, 2:4, rows, :] = lower
        else:
            kept[tile, 0:2, rows, :] = upper
            kept[tile, 2:4, rows, :] = lower
            copies[u][ZZ].start()

    def home(u):
        tile, part, start, height = units[u]
        rows = pl.ds(start, height)
        copies[u][ZZ].wait_recv()
        out[0, 0, :, rows, :] += z_in[:, rows, :]

    stages = {"product": product, "chip": chip, "forward": forward, "finish": finish, "home": home}
    for name, u in plan_steps(len(ROWS1), len(units)):
        stages[name](u)

    for copy in a_copies:
        copy.wait_send()
    a_table_copy.wait_send()
    c_list_copy.wait_send()
    for links in copies:
        for copy in links.values():
            copy.wait_send()


def solution(mesh):
    shape = tuple(mesh.shape[axis] for axis in ("row", "col", "layer"))

    def on_device(a_blocks, a_cells, a_count, b_blocks, b_cells, b_count, c_cells):
        cap_a, cap_b, cap_c = a_blocks.shape[3], b_blocks.shape[3], c_cells.shape[2]
        here = cap_c // shape[2]
        units = len(ROWS1) + len(ROWS2)
        bf16, f32, i32 = jnp.bfloat16, jnp.float32, jnp.int32
        vmem, smem, dma = pltpu.VMEM, pltpu.SMEM, pltpu.SemaphoreType.DMA
        pair = (2, here // 2, BS, BS)
        return pl.pallas_call(
            lambda *refs: kernel(shape, *refs),
            out_shape=jax.ShapeDtypeStruct((1, 1, here, BS, BS), f32),
            in_specs=[pl.BlockSpec(memory_space=pltpu.SMEM)] * 5 + [pl.BlockSpec(memory_space=pl.ANY)] * 2,
            out_specs=pl.BlockSpec(memory_space=pltpu.VMEM),
            scratch_shapes=[vmem((cap_a + 1, height, BS), bf16) for height in ROWS2] + [
                vmem((cap_a + 1, BS, BS), bf16),
                vmem((cap_b + 1, BS, BS), bf16),
                vmem((CR * max(ROWS1 + ROWS2), KW * BS), bf16),
                vmem((CC // 2, KW * BS, 2 * BS), bf16),
                vmem((CR * CC, max(ROWS1 + ROWS2), BS), f32),
                vmem((2, cap_c // 2, BS, BS), f32),
                vmem((2, cap_c // 2, BS, BS), f32),
                vmem((2, cap_c // 2, BS, BS), f32),
                vmem(pair, f32), vmem(pair, f32), vmem(pair, f32), vmem(pair, f32), vmem(pair, f32), vmem(pair, f32),
                vmem((here, BS, BS), f32),
                vmem((1, BS), i32), vmem((1, BS), i32), vmem((1, BS), i32), vmem((1, BS), i32), vmem((1, BS), i32),
                smem((1, BS), i32), smem((1, BS), i32), smem((1, BS), i32), smem((1, BS), i32),
                dma((6,)),
                dma((len(ROWS2),)), dma((len(ROWS2),)),
                dma((2,)), dma((2,)),
                dma((units, 8)), dma((units, 8)),
            ],
            compiler_params=pltpu.CompilerParams(
                collective_id=0, has_side_effects=True, vmem_limit_bytes=56 * 1024 * 1024
            ),
        )(a_cells, a_count, b_cells, b_count, c_cells, a_blocks, b_blocks)

    return jax.shard_map(
        on_device,
        mesh=mesh,
        in_specs=(
            P("row", "col", "layer", None, None, None),
            P("row", "col", "layer", None),
            P("row", "col", "layer"),
            P("row", "col", "layer", None, None, None),
            P("row", "col", "layer", None),
            P("row", "col", "layer"),
            P("row", "col", None),
        ),
        out_specs=P("row", "col", "layer", None, None),
        check_vma=False,
    )
```

```python
import jax
import jax.numpy as jnp
from jax import lax
from jax.experimental import pallas as pl
from jax.experimental.pallas import tpu as pltpu
from jax.sharding import PartitionSpec as P

CR = 4
CC = 16
KW = 8
BS = 128
ROWS1 = (64, 64)
ROWS2 = (48, 32, 32, 16)
DIRECT = (5,)
MESH = pl.DeviceIdType.MESH
CORE, FA, FB, DA, DB, SA, SB, ZZ = range(8)


def plan_units():
    units = []
    for tile, rows in enumerate((ROWS1, ROWS2)):
        start = 0
        for part, height in enumerate(rows):
            units.append((tile, part, start, height))
            start += height
    return units


STEPS = (
    ("product", 0), ("product", 1), ("chip", 0), ("send", 1), ("chip", 1), ("product", 2), ("send", 2),
    ("forward", 0), ("forward", 1), ("chip", 2), ("product", 3), ("send", 3), ("finish", 0), ("forward", 2),
    ("finish", 1), ("chip", 3), ("product", 4), ("forward", 3), ("finish", 2), ("chip", 4), ("product", 5),
    ("home", 2), ("finish", 3), ("chip", 5), ("forward", 4), ("home", 3), ("finish", 4), ("home", 5),
    ("home", 4),
)


def slot_table(cells, count, capacity):
    lanes = lax.broadcasted_iota(jnp.int32, (1, BS), 1)

    def place(s, table):
        cell = jnp.where(s < count, cells[0, 0, 0, s], -1)
        return jnp.where(lanes == cell, s, table)

    return lax.fori_loop(0, capacity, place, jnp.full((1, BS), capacity, jnp.int32), unroll=8)


def kernel(shape, a_cells, a_count, b_cells, b_count, c_cells, a_hbm, b_hbm, out, *scratch):
    n_row, n_col, n_layer = shape
    units = plan_units()
    parts = len(ROWS2)
    a_next = scratch[:parts]
    (a_own, b_slots, left, right, dense, kept, away, core_in,
     fa_in, fb_in, da_in, db_in, sa_in, sb_in, z_in, parts_in,
     a_table, b_table, c_list, a_table_in, c_list_in,
     a_at, b_at, a_next_at, c_next_at,
     local_sem, a_send, a_recv, int_send, int_recv, send_sem, recv_sem) = scratch[parts:]
    cap_a = a_hbm.shape[3]
    cap_b = b_hbm.shape[3]

    r, c, l = lax.axis_index("row"), lax.axis_index("col"), lax.axis_index("layer")
    ny = n_layer // 2
    y, p = l // 2, l % 2
    r_up, r_down = lax.rem(r + 1, n_row), lax.rem(r + n_row - 1, n_row)
    c_up, c_down = lax.rem(c + 1, n_col), lax.rem(c + n_col - 1, n_col)
    a_to, a_from = (r_down, c_up, l), (r_up, c_down, l)
    sibling = (r, c, y * 2 + 1 - p)
    y_up = (r, c, lax.rem(y + 1, ny) * 2 + p)
    y_down = (r, c, lax.rem(y + ny - 1, ny) * 2 + p)

    barrier = pltpu.get_barrier_semaphore()
    owners = [(r, c_down, lax.rem(y + e, ny) * 2 + p) for e in range(4)]
    sources = [(r, c_up, lax.rem(y + ny - e, ny) * 2 + p) for e in range(4)]
    others = (a_to, a_from, sibling, y_up, y_down, *owners, *sources)
    for other in others:
        pl.semaphore_signal(barrier, inc=1, device_id=other, device_id_type=MESH)

    b_copy = pltpu.make_async_copy(b_hbm.at[0, 0, 0], b_slots.at[pl.ds(0, cap_b)], local_sem.at[0])
    a_copy = pltpu.make_async_copy(a_hbm.at[0, 0, 0], a_own.at[pl.ds(0, cap_a)], local_sem.at[1])
    a_copy.start()
    b_copy.start()
    pl.semaphore_wait(barrier, len(others))

    def remote(src, dst, send, recv, device):
        return pltpu.make_async_remote_copy(
            src_ref=src, dst_ref=dst, send_sem=send, recv_sem=recv, device_id=device, device_id_type=MESH
        )

    a_copies = []
    for tile, part, start, height in units:
        if tile == 1:
            a_copies.append(
                remote(
                    a_hbm.at[0, 0, 0, :, pl.ds(start, height), :],
                    a_next[part].at[pl.ds(0, cap_a)],
                    a_send.at[part],
                    a_recv.at[part],
                    a_to,
                )
            )
    a_copies[0].start()

    lanes = lax.broadcasted_iota(jnp.int32, (1, BS), 1)

    def list_cell(t, row):
        return jnp.where(lanes == t, c_cells[0, 0, t], row)

    a_table[...] = slot_table(a_cells, a_count[0, 0, 0], cap_a)
    a_at_copy = pltpu.make_async_copy(a_table, a_at, local_sem.at[2])
    a_at_copy.start()
    b_table[...] = slot_table(b_cells, b_count[0, 0, 0], cap_b)
    b_at_copy = pltpu.make_async_copy(b_table, b_at, local_sem.at[3])
    b_at_copy.start()
    a_table_copy = remote(a_table, a_table_in, int_send.at[0], int_recv.at[0], a_to)
    a_table_copy.start()
    c_list[...] = lax.fori_loop(0, c_cells.shape[2], list_cell, jnp.zeros((1, BS), jnp.int32), unroll=8)
    c_list_copy = remote(c_list, c_list_in, int_send.at[1], int_recv.at[1], sources[0])
    c_list_copy.start()

    a_own[cap_a] = jnp.zeros((BS, BS), a_own.dtype)
    b_slots[cap_b] = jnp.zeros((BS, BS), b_slots.dtype)
    for tile, part, start, height in units:
        if tile == 1:
            a_next[part][cap_a] = jnp.zeros((height, BS), a_own.dtype)

    b_at_copy.wait()
    b_copy.wait()

    @pl.loop(0, KW)
    def _(k):
        for j in range(CC):
            right[j // 2, pl.ds(k * BS, BS), (j % 2) * BS:(j % 2 + 1) * BS] = b_slots[b_at[0, k * CC + j]]

    a_at_copy.wait()
    a_copy.wait()

    a_next_at_copy = pltpu.make_async_copy(a_table_in, a_next_at, local_sem.at[4])
    c_next_at_copy = pltpu.make_async_copy(c_list_in, c_next_at, local_sem.at[5])

    def copies_of(u):
        tile, part, start, height = units[u]
        rows = pl.ds(start, height)

        def link(kind, src, dst, device):
            return remote(src, dst, send_sem.at[u, kind], recv_sem.at[u, kind], device)

        def blocks(first, count):
            return kept.at[tile, pl.ds(first, count), rows, :]

        if u in DIRECT:
            base = start - units[DIRECT[0]][2]
            links = {
                1 + e: link(1 + e, blocks(4 * e, 4), parts_in.at[e, :, pl.ds(base, height), :], owners[e])
                for e in range(4)
            }
            links[CORE] = link(CORE, away.at[tile, :, rows, :], core_in.at[tile, :, rows, :], sibling)
            return links
        links = {
            CORE: link(CORE, away.at[tile, :, rows, :], core_in.at[tile, :, rows, :], sibling),
            FA: link(FA, blocks(8, 2), fa_in.at[tile, :, rows, :], y_up),
            FB: link(FB, blocks(10, 2), fb_in.at[tile, :, rows, :], y_down),
            DB: link(DB, blocks(6, 2), db_in.at[tile, :, rows, :], y_up),
            DA: link(DA, blocks(12, 2), da_in.at[tile, :, rows, :], y_down),
            SA: link(SA, blocks(4, 2), sa_in.at[tile, :, rows, :], y_up),
            SB: link(SB, blocks(14, 2), sb_in.at[tile, :, rows, :], y_down),
        }
        if tile == 1:
            links[ZZ] = link(ZZ, blocks(0, 4), z_in.at[:, rows, :], owners[0])
        return links

    copies = [copies_of(u) for u in range(len(units))]

    def product(u):
        tile, part, start, height = units[u]
        rows = pl.ds(start, height)
        if tile == 1:
            if part == 0:
                a_table_copy.wait_recv()
                a_next_at_copy.start()
                c_list_copy.wait_recv()
                c_next_at_copy.start()
                a_next_at_copy.wait()
                c_next_at_copy.wait()
            a_copies[part].wait_recv()
        for i in range(CR):
            for k in range(KW):
                if tile == 0:
                    block = a_own[a_at[0, i * KW + k], rows, :]
                else:
                    block = a_next[part][a_next_at[0, i * KW + k]]
                left[i * height:(i + 1) * height, k * BS:(k + 1) * BS] = block

        @pl.loop(0, CC // 2)
        def _(j):
            total = jnp.dot(left[0:CR * height, :], right[j], preferred_element_type=jnp.float32)
            for i in range(CR):
                for s in range(2):
                    dense[i * CC + 2 * j + s, 0:height, :] = total[i * height:(i + 1) * height, s * BS:(s + 1) * BS]

        @pl.loop(0, ny)
        def _(e):
            base = lax.rem(y + e, ny) * 8
            for q in range(4):
                for ours, target in ((False, away), (True, kept)):
                    t = base + (p if ours else 1 - p) * 4 + q
                    cell = c_cells[0, 0, t] if tile == 0 else c_next_at[0, t]
                    target[tile, e * 4 + q, rows, :] = dense[cell, 0:height, :]

        copies[u][CORE].start()

    def chip(u):
        tile, part, start, height = units[u]
        rows = pl.ds(start, height)
        copies[u][CORE].wait_recv()
        for e, sends in ((2, (FA, FB)), (1, (DB,)), (3, (DA,)), (0, ())):
            span = slice(e * 4, e * 4 + 4)
            kept[tile, span, rows, :] += core_in[tile, span, rows, :]
            for kind in (1 + e,) if u in DIRECT else sends:
                copies[u][kind].start()

    def forward(u):
        tile, part, start, height = units[u]
        rows = pl.ds(start, height)
        for came, sent, first, arrived in ((FA, SA, 4, fa_in), (FB, SB, 14, fb_in)):
            copies[u][came].wait_recv()
            kept[tile, first:first + 2, rows, :] += arrived[tile, :, rows, :]
            copies[u][sent].start()

    def finish(u):
        tile, part, start, height = units[u]
        rows = pl.ds(start, height)
        for kind in (DA, DB, SA, SB):
            copies[u][kind].wait_recv()
        upper = kept[tile, 0:2, rows, :] + da_in[tile, :, rows, :] + sa_in[tile, :, rows, :]
        lower = kept[tile, 2:4, rows, :] + db_in[tile, :, rows, :] + sb_in[tile, :, rows, :]
        if tile == 0:
            out[0, 0, 0:2, rows, :] = upper
            out[0, 0, 2:4, rows, :] = lower
        else:
            kept[tile, 0:2, rows, :] = upper
            kept[tile, 2:4, rows, :] = lower
            copies[u][ZZ].start()

    def home(u):
        tile, part, start, height = units[u]
        rows = pl.ds(start, height)
        if u in DIRECT:
            near = pl.ds(start - units[DIRECT[0]][2], height)
            for e in range(4):
                copies[u][1 + e].wait_recv()
            out[0, 0, :, rows, :] += (parts_in[0, :, near, :] + parts_in[1, :, near, :]) + (
                parts_in[2, :, near, :] + parts_in[3, :, near, :]
            )
        else:
            copies[u][ZZ].wait_recv()
            out[0, 0, :, rows, :] += z_in[:, rows, :]

    def send(part):
        a_copies[part - 1].wait_send()
        a_copies[part].start()

    stages = {"send": send, "product": product, "chip": chip, "forward": forward, "finish": finish, "home": home}
    for name, u in STEPS:
        stages[name](u)

    a_copies[-1].wait_send()
    a_table_copy.wait_send()
    c_list_copy.wait_send()
    for links in copies:
        for copy in links.values():
            copy.wait_send()


def solution(mesh):
    shape = tuple(mesh.shape[axis] for axis in ("row", "col", "layer"))

    def on_device(a_blocks, a_cells, a_count, b_blocks, b_cells, b_count, c_cells):
        cap_a, cap_b, cap_c = a_blocks.shape[3], b_blocks.shape[3], c_cells.shape[2]
        here = cap_c // shape[2]
        units = len(ROWS1) + len(ROWS2)
        bf16, f32, i32 = jnp.bfloat16, jnp.float32, jnp.int32
        vmem, smem, dma = pltpu.VMEM, pltpu.SMEM, pltpu.SemaphoreType.DMA
        pair = (2, here // 2, BS, BS)
        return pl.pallas_call(
            lambda *refs: kernel(shape, *refs),
            out_shape=jax.ShapeDtypeStruct((1, 1, here, BS, BS), f32),
            in_specs=[pl.BlockSpec(memory_space=pltpu.SMEM)] * 5 + [pl.BlockSpec(memory_space=pl.ANY)] * 2,
            out_specs=pl.BlockSpec(memory_space=pltpu.VMEM),
            scratch_shapes=[vmem((cap_a + 1, height, BS), bf16) for height in ROWS2] + [
                vmem((cap_a + 1, BS, BS), bf16),
                vmem((cap_b + 1, BS, BS), bf16),
                vmem((CR * max(ROWS1 + ROWS2), KW * BS), bf16),
                vmem((CC // 2, KW * BS, 2 * BS), bf16),
                vmem((CR * CC, max(ROWS1 + ROWS2), BS), f32),
                vmem((2, cap_c // 2, BS, BS), f32),
                vmem((2, cap_c // 2, BS, BS), f32),
                vmem((2, cap_c // 2, BS, BS), f32),
                vmem(pair, f32), vmem(pair, f32), vmem(pair, f32), vmem(pair, f32), vmem(pair, f32), vmem(pair, f32),
                vmem((here, BS, BS), f32),
                vmem((4, here, sum(ROWS2[u - len(ROWS1)] for u in DIRECT), BS), f32),
                vmem((1, BS), i32), vmem((1, BS), i32), vmem((1, BS), i32), vmem((1, BS), i32), vmem((1, BS), i32),
                smem((1, BS), i32), smem((1, BS), i32), smem((1, BS), i32), smem((1, BS), i32),
                dma((6,)),
                dma((len(ROWS2),)), dma((len(ROWS2),)),
                dma((2,)), dma((2,)),
                dma((units, 8)), dma((units, 8)),
            ],
            compiler_params=pltpu.CompilerParams(
                collective_id=0, has_side_effects=True, vmem_limit_bytes=56 * 1024 * 1024
            ),
        )(a_cells, a_count, b_cells, b_count, c_cells, a_blocks, b_blocks)

    return jax.shard_map(
        on_device,
        mesh=mesh,
        in_specs=(
            P("row", "col", "layer", None, None, None),
            P("row", "col", "layer", None),
            P("row", "col", "layer"),
            P("row", "col", "layer", None, None, None),
            P("row", "col", "layer", None),
            P("row", "col", "layer"),
            P("row", "col", None),
        ),
        out_specs=P("row", "col", "layer", None, None),
        check_vma=False,
    )
```

```python
import jax
import jax.numpy as jnp
from jax import lax
from jax.experimental import pallas as pl
from jax.experimental.pallas import tpu as pltpu
from jax.sharding import PartitionSpec as P

CR = 4
CC = 16
KW = 8
BS = 128
ROWS1 = (64, 64)
ROWS2 = (48, 32, 32, 16)
DIRECT = (5,)
MESH = pl.DeviceIdType.MESH
CORE, FA, FB, DA, DB, SA, SB, ZZ = range(8)


def plan_units():
    units = []
    for tile, rows in enumerate((ROWS1, ROWS2)):
        start = 0
        for part, height in enumerate(rows):
            units.append((tile, part, start, height))
            start += height
    return units


STEPS = (
    ("product", 0), ("product", 1), ("chip", 0), ("send", 1), ("chip", 1), ("product", 2), ("send", 2),
    ("forward", 0), ("forward", 1), ("chip", 2), ("product", 3), ("send", 3), ("finish", 0), ("forward", 2),
    ("finish", 1), ("chip", 3), ("product", 4), ("forward", 3), ("finish", 2), ("chip", 4), ("product", 5),
    ("home", 2), ("finish", 3), ("chip", 5), ("forward", 4), ("home", 3), ("finish", 4), ("home", 5),
    ("home", 4),
)


def slot_table(cells, count, capacity):
    lanes = lax.broadcasted_iota(jnp.int32, (1, BS), 1)

    def place(s, table):
        cell = jnp.where(s < count, cells[0, 0, 0, s], -1)
        return jnp.where(lanes == cell, s, table)

    return lax.fori_loop(0, capacity, place, jnp.full((1, BS), capacity, jnp.int32), unroll=8)


def kernel(shape, a_cells, a_count, b_cells, b_count, c_cells, a_hbm, b_hbm, out, *scratch):
    n_row, n_col, n_layer = shape
    units = plan_units()
    parts = len(ROWS2)
    a_next = scratch[:parts]
    (a_own, b_slots, left, right, dense, kept, away, core_in,
     fa_in, fb_in, da_in, db_in, sa_in, sb_in, z_in, parts_in,
     a_table, b_table, c_list, a_table_in, c_list_in,
     a_at, b_at, a_next_at, c_next_at,
     local_sem, a_send, a_recv, int_send, int_recv, send_sem, recv_sem) = scratch[parts:]
    cap_a = a_hbm.shape[3]
    cap_b = b_hbm.shape[3]

    r, c, l = lax.axis_index("row"), lax.axis_index("col"), lax.axis_index("layer")
    ny = n_layer // 2
    y, p = l // 2, l % 2
    r_up, r_down = lax.rem(r + 1, n_row), lax.rem(r + n_row - 1, n_row)
    c_up, c_down = lax.rem(c + 1, n_col), lax.rem(c + n_col - 1, n_col)
    a_to, a_from = (r_down, c_up, l), (r_up, c_down, l)
    sibling = (r, c, y * 2 + 1 - p)
    y_up = (r, c, lax.rem(y + 1, ny) * 2 + p)
    y_down = (r, c, lax.rem(y + ny - 1, ny) * 2 + p)

    barrier = pltpu.get_barrier_semaphore()
    owners = [(r, c_down, lax.rem(y + e, ny) * 2 + p) for e in range(4)]
    sources = [(r, c_up, lax.rem(y + ny - e, ny) * 2 + p) for e in range(4)]
    others = (a_to, a_from, sibling, y_up, y_down, *owners, *sources)
    for other in others:
        pl.semaphore_signal(barrier, inc=1, device_id=other, device_id_type=MESH)

    b_copy = pltpu.make_async_copy(b_hbm.at[0, 0, 0], b_slots.at[pl.ds(0, cap_b)], local_sem.at[0])
    a_copy = pltpu.make_async_copy(a_hbm.at[0, 0, 0], a_own.at[pl.ds(0, cap_a)], local_sem.at[1])
    a_copy.start()
    b_copy.start()
    pl.semaphore_wait(barrier, len(others))

    def remote(src, dst, send, recv, device):
        return pltpu.make_async_remote_copy(
            src_ref=src, dst_ref=dst, send_sem=send, recv_sem=recv, device_id=device, device_id_type=MESH
        )

    a_copies = []
    for tile, part, start, height in units:
        if tile == 1:
            a_copies.append(
                remote(
                    a_hbm.at[0, 0, 0, :, pl.ds(start, height), :],
                    a_next[part].at[pl.ds(0, cap_a)],
                    a_send.at[part],
                    a_recv.at[part],
                    a_to,
                )
            )
    a_copies[0].start()

    lanes = lax.broadcasted_iota(jnp.int32, (1, BS), 1)

    def list_cell(t, row):
        return jnp.where(lanes == t, c_cells[0, 0, t], row)

    a_table[...] = slot_table(a_cells, a_count[0, 0, 0], cap_a)
    a_at_copy = pltpu.make_async_copy(a_table, a_at, local_sem.at[2])
    a_at_copy.start()
    b_table[...] = slot_table(b_cells, b_count[0, 0, 0], cap_b)
    b_at_copy = pltpu.make_async_copy(b_table, b_at, local_sem.at[3])
    b_at_copy.start()
    a_table_copy = remote(a_table, a_table_in, int_send.at[0], int_recv.at[0], a_to)
    a_table_copy.start()
    c_list[...] = lax.fori_loop(0, c_cells.shape[2], list_cell, jnp.zeros((1, BS), jnp.int32), unroll=8)
    c_list_copy = remote(c_list, c_list_in, int_send.at[1], int_recv.at[1], sources[0])
    c_list_copy.start()

    a_own[cap_a] = jnp.zeros((BS, BS), a_own.dtype)
    b_slots[cap_b] = jnp.zeros((BS, BS), b_slots.dtype)
    for tile, part, start, height in units:
        if tile == 1:
            a_next[part][cap_a] = jnp.zeros((height, BS), a_own.dtype)

    b_at_copy.wait()
    b_copy.wait()

    @pl.loop(0, KW)
    def _(k):
        for j in range(CC):
            right[j // 2, pl.ds(k * BS, BS), (j % 2) * BS:(j % 2 + 1) * BS] = b_slots[b_at[0, k * CC + j]]

    a_at_copy.wait()
    a_copy.wait()

    a_next_at_copy = pltpu.make_async_copy(a_table_in, a_next_at, local_sem.at[4])
    c_next_at_copy = pltpu.make_async_copy(c_list_in, c_next_at, local_sem.at[5])

    def copies_of(u):
        tile, part, start, height = units[u]
        rows = pl.ds(start, height)

        def link(kind, src, dst, device):
            return remote(src, dst, send_sem.at[u, kind], recv_sem.at[u, kind], device)

        def blocks(first, count):
            return kept.at[tile, pl.ds(first, count), rows, :]

        if u in DIRECT:
            base = start - units[DIRECT[0]][2]
            links = {
                1 + e: link(1 + e, blocks(4 * e, 4), parts_in.at[e, :, pl.ds(base, height), :], owners[e])
                for e in range(4)
            }
            links[CORE] = link(CORE, away.at[tile, :, rows, :], core_in.at[tile, :, rows, :], sibling)
            return links
        links = {
            CORE: link(CORE, away.at[tile, :, rows, :], core_in.at[tile, :, rows, :], sibling),
            FA: link(FA, blocks(8, 2), fa_in.at[tile, :, rows, :], y_up),
            FB: link(FB, blocks(10, 2), fb_in.at[tile, :, rows, :], y_down),
            DB: link(DB, blocks(6, 2), db_in.at[tile, :, rows, :], y_up),
            DA: link(DA, blocks(12, 2), da_in.at[tile, :, rows, :], y_down),
            SA: link(SA, blocks(4, 2), sa_in.at[tile, :, rows, :], y_up),
            SB: link(SB, blocks(14, 2), sb_in.at[tile, :, rows, :], y_down),
        }
        if tile == 1:
            links[ZZ] = link(ZZ, blocks(0, 4), z_in.at[:, rows, :], owners[0])
        return links

    copies = [copies_of(u) for u in range(len(units))]

    def product(u):
        tile, part, start, height = units[u]
        rows = pl.ds(start, height)
        if tile == 1:
            if part == 0:
                a_table_copy.wait_recv()
                a_next_at_copy.start()
                c_list_copy.wait_recv()
                c_next_at_copy.start()
                a_next_at_copy.wait()
                c_next_at_copy.wait()
            a_copies[part].wait_recv()
        for i in range(CR):
            for k in range(KW):
                if tile == 0:
                    block = a_own[a_at[0, i * KW + k], rows, :]
                else:
                    block = a_next[part][a_next_at[0, i * KW + k]]
                left[i * height:(i + 1) * height, k * BS:(k + 1) * BS] = block

        @pl.loop(0, CC // 2, unroll=2)
        def _(j):
            total = jnp.dot(left[0:CR * height, :], right[j], preferred_element_type=jnp.float32)
            for i in range(CR):
                for s in range(2):
                    dense[i * CC + 2 * j + s, 0:height, :] = total[i * height:(i + 1) * height, s * BS:(s + 1) * BS]

        @pl.loop(0, ny)
        def _(e):
            base = lax.rem(y + e, ny) * 8
            for q in range(4):
                for ours, target in ((False, away), (True, kept)):
                    t = base + (p if ours else 1 - p) * 4 + q
                    cell = c_cells[0, 0, t] if tile == 0 else c_next_at[0, t]
                    target[tile, e * 4 + q, rows, :] = dense[cell, 0:height, :]

        copies[u][CORE].start()

    def chip(u):
        tile, part, start, height = units[u]
        rows = pl.ds(start, height)
        copies[u][CORE].wait_recv()
        for e, sends in ((2, (FA, FB)), (1, (DB,)), (3, (DA,)), (0, ())):
            span = slice(e * 4, e * 4 + 4)
            kept[tile, span, rows, :] += core_in[tile, span, rows, :]
            for kind in (1 + e,) if u in DIRECT else sends:
                copies[u][kind].start()

    def forward(u):
        tile, part, start, height = units[u]
        rows = pl.ds(start, height)
        for came, sent, first, arrived in ((FA, SA, 4, fa_in), (FB, SB, 14, fb_in)):
            copies[u][came].wait_recv()
            kept[tile, first:first + 2, rows, :] += arrived[tile, :, rows, :]
            copies[u][sent].start()

    def finish(u):
        tile, part, start, height = units[u]
        rows = pl.ds(start, height)
        for kind in (DA, DB, SA, SB):
            copies[u][kind].wait_recv()
        upper = kept[tile, 0:2, rows, :] + da_in[tile, :, rows, :] + sa_in[tile, :, rows, :]
        lower = kept[tile, 2:4, rows, :] + db_in[tile, :, rows, :] + sb_in[tile, :, rows, :]
        if tile == 0:
            out[0, 0, 0:2, rows, :] = upper
            out[0, 0, 2:4, rows, :] = lower
        else:
            kept[tile, 0:2, rows, :] = upper
            kept[tile, 2:4, rows, :] = lower
            copies[u][ZZ].start()

    def home(u):
        tile, part, start, height = units[u]
        rows = pl.ds(start, height)
        if u in DIRECT:
            near = pl.ds(start - units[DIRECT[0]][2], height)
            for e in range(4):
                copies[u][1 + e].wait_recv()
            out[0, 0, :, rows, :] += (parts_in[0, :, near, :] + parts_in[1, :, near, :]) + (
                parts_in[2, :, near, :] + parts_in[3, :, near, :]
            )
        else:
            copies[u][ZZ].wait_recv()
            out[0, 0, :, rows, :] += z_in[:, rows, :]

    def send(part):
        a_copies[part - 1].wait_send()
        a_copies[part].start()

    stages = {"send": send, "product": product, "chip": chip, "forward": forward, "finish": finish, "home": home}
    for name, u in STEPS:
        stages[name](u)

    a_copies[-1].wait_send()
    a_table_copy.wait_send()
    c_list_copy.wait_send()
    for links in copies:
        for copy in links.values():
            copy.wait_send()


def solution(mesh):
    shape = tuple(mesh.shape[axis] for axis in ("row", "col", "layer"))

    def on_device(a_blocks, a_cells, a_count, b_blocks, b_cells, b_count, c_cells):
        cap_a, cap_b, cap_c = a_blocks.shape[3], b_blocks.shape[3], c_cells.shape[2]
        here = cap_c // shape[2]
        units = len(ROWS1) + len(ROWS2)
        bf16, f32, i32 = jnp.bfloat16, jnp.float32, jnp.int32
        vmem, smem, dma = pltpu.VMEM, pltpu.SMEM, pltpu.SemaphoreType.DMA
        pair = (2, here // 2, BS, BS)
        return pl.pallas_call(
            lambda *refs: kernel(shape, *refs),
            out_shape=jax.ShapeDtypeStruct((1, 1, here, BS, BS), f32),
            in_specs=[pl.BlockSpec(memory_space=pltpu.SMEM)] * 5 + [pl.BlockSpec(memory_space=pl.ANY)] * 2,
            out_specs=pl.BlockSpec(memory_space=pltpu.VMEM),
            scratch_shapes=[vmem((cap_a + 1, height, BS), bf16) for height in ROWS2] + [
                vmem((cap_a + 1, BS, BS), bf16),
                vmem((cap_b + 1, BS, BS), bf16),
                vmem((CR * max(ROWS1 + ROWS2), KW * BS), bf16),
                vmem((CC // 2, KW * BS, 2 * BS), bf16),
                vmem((CR * CC, max(ROWS1 + ROWS2), BS), f32),
                vmem((2, cap_c // 2, BS, BS), f32),
                vmem((2, cap_c // 2, BS, BS), f32),
                vmem((2, cap_c // 2, BS, BS), f32),
                vmem(pair, f32), vmem(pair, f32), vmem(pair, f32), vmem(pair, f32), vmem(pair, f32), vmem(pair, f32),
                vmem((here, BS, BS), f32),
                vmem((4, here, sum(ROWS2[u - len(ROWS1)] for u in DIRECT), BS), f32),
                vmem((1, BS), i32), vmem((1, BS), i32), vmem((1, BS), i32), vmem((1, BS), i32), vmem((1, BS), i32),
                smem((1, BS), i32), smem((1, BS), i32), smem((1, BS), i32), smem((1, BS), i32),
                dma((6,)),
                dma((len(ROWS2),)), dma((len(ROWS2),)),
                dma((2,)), dma((2,)),
                dma((units, 8)), dma((units, 8)),
            ],
            compiler_params=pltpu.CompilerParams(
                collective_id=0, has_side_effects=True, vmem_limit_bytes=56 * 1024 * 1024
            ),
        )(a_cells, a_count, b_cells, b_count, c_cells, a_blocks, b_blocks)

    return jax.shard_map(
        on_device,
        mesh=mesh,
        in_specs=(
            P("row", "col", "layer", None, None, None),
            P("row", "col", "layer", None),
            P("row", "col", "layer"),
            P("row", "col", "layer", None, None, None),
            P("row", "col", "layer", None),
            P("row", "col", "layer"),
            P("row", "col", None),
        ),
        out_specs=P("row", "col", "layer", None, None),
        check_vma=False,
    )
```
